256 devices in a mesh: row: 64 (over y_lo, z, x), rep: 4 (over y_hi, core).
Axes of the slice: x: 4, y: 4 (y_hi: 2, y_lo: 2; y = y_hi * 2 + y_lo), z: 8, core: 2. Of those that a mesh axis runs over, the one named last changes fastest.
Arguments:
- features: bfloat16 [262144, 256], P(('row', 'rep')), may hold values from -6 to 6
- weight: bfloat16 [256, 256], replicated, may hold values from -0.375 to 0.375
- cotangent: bfloat16 [262144, 256], P(('row', 'rep')), may hold values from -6 to 6
- group_tiles: bfloat16 [256, 4, 8, 4, 128, 128], P(('row', 'rep')), may hold values from -0.125 to 0.125
- group_src: int32 [256, 4, 8, 4], P(('row', 'rep')), may hold values from 0 to 7, as said below
- group_wt: int32 [256, 4, 8, 4], P(('row', 'rep')), may hold values from 1 to 8
- remote_tiles: bfloat16 [256, 64, 128, 128], P(('row', 'rep')), may hold values from -0.125 to 0.125
- remote_src: int32 [256, 64], P(('row', 'rep')), may hold values from 0 to 7
- remote_wt: int32 [256, 64], P(('row', 'rep')), may hold values from 0 to 8
- incoming_dst: int32 [256, 64], P(('row', 'rep')), may hold values from 0 to 7
Outputs:
- output: bfloat16 [262144, 256], P(('row', 'rep'))
- grad_weight: float32 [256, 256], replicated
- grad_feat: bfloat16 [262144, 256], P(('row', 'rep'))
The draws below stay inside these ranges and needn't reach their ends.
Inputs may be any that keep to these rules, and one draw needn't show every extreme that they name: `group_src`: for each device, source device and destination block the 4 source blocks are distinct.
All inputs are finite; a program needn't handle non-finite values.
Results may differ from the reference program's by a relative error of at most 0.0061.
Values may be sent and summed in bfloat16 or wider, within the bound.
No kernel may reach another device: no remote copies, remote signals or barrier semaphores. Data moves between devices by JAX's collectives and lax.ppermute only.
A program may use at most 128 MiB of HBM per device.

```python
import math
import jax
import jax.numpy as jnp
from jax import lax

F = 256
TILE = 128
SRC_PER = 4
BLK_DEV = 8
DEVS = 256
NODES = 262144
N_ROW = 64
N_REP = 4


def draw_group_src(key, part):
    key = jax.random.fold_in(key, 11)
    scores = jax.random.randint(key, (DEVS, N_REP, BLK_DEV, BLK_DEV), 0, 1 << 20, dtype=jnp.int32)
    scores = scores * BLK_DEV + jnp.arange(BLK_DEV, dtype=jnp.int32)
    ranking = jnp.argsort(scores, axis=-1, stable=True).astype(jnp.int32)
    return ranking[..., :SRC_PER]


def plant(array, stream_key, least, high):
    shape = array.shape
    spot = [jax.random.randint(jax.random.fold_in(stream_key, axis), (), 0, shape[axis]) for axis in range(len(shape))]
    array = array.at[tuple(spot)].set(least)
    longest = shape.index(max(shape))
    spot[longest] = (spot[longest] + 1) % shape[longest]
    return array.at[tuple(spot)].set(high)


def block_levels(own_key, shape, pieces, smallest, top_value):
    def one(dim, shards_of):
        draws = jax.random.uniform(jax.random.fold_in(jax.random.fold_in(own_key, 6), dim), (shards_of,), jnp.float32, smallest / len(pieces), top_value / len(pieces))
        return jnp.repeat(jnp.exp(draws), shape[dim] // shards_of).reshape((-1,) + (1,) * (len(shape) - dim - 1))

    loudness = one(*pieces[0])
    for cut in pieces[1:]:
        loudness = loudness * one(*cut)
    return loudness


def gaussian(own_key, dims, deviation, reach, shards=(), kind=jnp.bfloat16):
    array = jax.random.normal(own_key, dims, jnp.float32) * deviation
    if len(shards) > 0:
        array = block_levels(own_key, dims, shards, -0.22, 0.18) * array
    return jnp.clip(array, min=-reach, max=reach).astype(kind)


def setup_inputs(seed: int = 0) -> dict:
    keys = jax.random.split(jax.random.key(seed), 11)
    features = gaussian(keys[0], (NODES, F), 1.0, 6.0, ((0, 256),))
    weight = gaussian(keys[1], (F, F), F ** -0.5, 0.375)
    cotangent = gaussian(keys[2], (NODES, F), 1.0, 6.0, ((0, 256),))
    group_tiles = gaussian(keys[3], (DEVS, N_REP, BLK_DEV, SRC_PER, TILE, TILE), (TILE * SRC_PER * N_REP) ** -0.5, 0.125, ((0, 256),))
    group_src = draw_group_src(jax.random.fold_in(keys[10], 71), 0)
    group_wt = plant(jax.random.randint(keys[5], (DEVS, N_REP, BLK_DEV, SRC_PER), 1, 9), jax.random.fold_in(keys[5], 1), 1, 8).astype(jnp.int32)
    remote_tiles = gaussian(keys[6], (DEVS, N_ROW, TILE, TILE), (TILE * N_ROW * 2 // BLK_DEV) ** -0.5, 0.125, ((0, 256),))
    remote_src = plant(jax.random.randint(keys[7], (DEVS, N_ROW), 0, BLK_DEV), jax.random.fold_in(keys[7], 1), 0, BLK_DEV - 1).astype(jnp.int32)
    remote_wt = plant(jax.random.randint(keys[8], (DEVS, N_ROW), 0, 9), jax.random.fold_in(keys[8], 1), 0, 8).astype(jnp.int32)
    incoming_dst = plant(jax.random.randint(keys[9], (DEVS, N_ROW), 0, BLK_DEV), jax.random.fold_in(keys[9], 1), 0, BLK_DEV - 1).astype(jnp.int32)
    return dict(features=features, weight=weight, cotangent=cotangent, group_tiles=group_tiles, group_src=group_src, group_wt=group_wt, remote_tiles=remote_tiles, remote_src=remote_src, remote_wt=remote_wt, incoming_dst=incoming_dst)


def reference(features, weight, cotangent, group_tiles, group_src, group_wt, remote_tiles, remote_src, remote_wt, incoming_dst):
    all_blocks = features.reshape(DEVS, BLK_DEV, TILE, F)
    devices = jnp.arange(DEVS, dtype=jnp.int32)
    block_ids = jnp.arange(BLK_DEV, dtype=jnp.int32)
    rep_ids = jnp.arange(N_REP, dtype=jnp.int32)
    row_ids = jnp.arange(N_ROW, dtype=jnp.int32)

    def forward_one(device):
        row_index = device // N_REP
        rep_index = device % N_REP
        row_feats = lax.dynamic_slice_in_dim(all_blocks, (row_index * N_REP).astype(jnp.int32), N_REP, 0)
        sources = group_src[device]
        scales = group_wt[device].astype(jnp.float32) / 8.0
        picked = jax.vmap(lambda block_set, index_set: jnp.take(block_set, index_set, axis=0))(row_feats, sources)
        products = jnp.einsum('qipab,qipbf->qipaf', group_tiles[device].astype(jnp.float32), picked.astype(jnp.float32))
        summed = lax.optimization_barrier(jnp.sum(products * scales[..., None, None], axis=(0, 2)))
        senders = row_ids * N_REP + rep_index
        far_tiles = remote_tiles[senders, row_index]
        far_src = remote_src[senders, row_index]
        far_scale = remote_wt[senders, row_index].astype(jnp.float32) / 8.0
        far_feats = all_blocks[senders, far_src]
        partial_value = (jnp.einsum('sab,sbf->saf', far_tiles.astype(jnp.float32), far_feats.astype(jnp.float32)) * far_scale[:, None, None]).astype(jnp.bfloat16)
        onehot = (incoming_dst[device][:, None] == block_ids[None, :]).astype(jnp.float32)
        summed = summed + jnp.einsum('sj,saf->jaf', onehot, partial_value.astype(jnp.float32), precision=lax.Precision.HIGHEST)
        return summed
    aggregate = lax.map(forward_one, devices).reshape(NODES, F).astype(jnp.bfloat16)
    preact = jnp.dot(aggregate, weight, preferred_element_type=jnp.float32)
    output = jax.nn.silu(preact).astype(jnp.bfloat16)
    sigmoid_pre = jax.nn.sigmoid(preact)
    grad_pre = (cotangent.astype(jnp.float32) * sigmoid_pre * (1.0 + preact * (1.0 - sigmoid_pre))).astype(jnp.bfloat16)
    grad_weight = jnp.dot(aggregate.T, grad_pre, preferred_element_type=jnp.float32) / math.sqrt(NODES)
    grad_agg = jnp.dot(grad_pre, weight.T, preferred_element_type=jnp.float32).astype(jnp.bfloat16)
    grad_blocks = grad_agg.reshape(DEVS, BLK_DEV, TILE, F)

    def backward_one(device):
        row_index = device // N_REP
        rep_index = device % N_REP
        holders = row_index * N_REP + rep_ids
        held_tiles = group_tiles[holders, rep_index]
        held_src = group_src[holders, rep_index]
        held_scale = group_wt[holders, rep_index].astype(jnp.float32) / 8.0
        grads_held = grad_blocks[holders]
        products = jnp.einsum('cipab,ciaf->cipbf', held_tiles.astype(jnp.float32), grads_held.astype(jnp.float32)) * held_scale[..., None, None]
        onehot = (held_src[..., None] == block_ids).astype(jnp.float32)
        summed = jnp.einsum('cipj,cipbf->jbf', onehot, products, precision=lax.Precision.HIGHEST)
        owners = row_ids * N_REP + rep_index
        owner_blocks = incoming_dst[owners, row_index]
        grads_far = grad_blocks[owners, owner_blocks]
        far_scale = remote_wt[device].astype(jnp.float32) / 8.0
        far_products = jnp.einsum('sab,saf->sbf', remote_tiles[device].astype(jnp.float32), grads_far.astype(jnp.float32)) * far_scale[:, None, None]
        onehot_far = (remote_src[device][:, None] == block_ids[None, :]).astype(jnp.float32)
        summed = summed + jnp.einsum('sj,sbf->jbf', onehot_far, far_products, precision=lax.Precision.HIGHEST)
        return summed
    grad_feat = lax.map(backward_one, devices).reshape(NODES, F).astype(jnp.bfloat16)
    return (output, grad_weight, grad_feat)
```

```python
import functools
import math

import jax
import jax.numpy as jnp
from jax import lax
from jax.experimental import pallas as pl
from jax.experimental.pallas import tpu as pltpu
from jax.sharding import Mesh, PartitionSpec as P

AXES = ("ylo", "z", "x", "yhi", "core")
SIZES = (2, 8, 4, 2, 2)
YLO, NZ, NX = 2, 8, 4
SIDE = YLO * NX
BLOCKS, TILE, FEAT = 8, 128, 256
BF16, F32 = jnp.bfloat16, jnp.float32
VMEM = pl.BlockSpec(memory_space=pltpu.VMEM)
SMEM = pl.BlockSpec(memory_space=pltpu.SMEM)
ANY = pl.BlockSpec(memory_space=pl.ANY)
BLOCK_SET = (BLOCKS, TILE, FEAT)
SLICE = FEAT // SIDE
PARAMS = pltpu.CompilerParams(vmem_limit_bytes=24 * 1024 * 1024)


def dot(left, right):
    return jnp.dot(left, right, preferred_element_type=F32)


def dot_t(left, right):
    return lax.dot_general(left, right, (((0,), (0,)), ((), ())), preferred_element_type=F32)


def cost(microseconds):
    return pl.CostEstimate(
        flops=int(microseconds * 1e9), bytes_accessed=1024, transcendentals=0
    )


def wrapped(value):
    return lax.rem(value + NZ, NZ)


def shape(dims, dtype=BF16):
    return jax.ShapeDtypeStruct(dims, dtype)


def sems(*dims):
    return pltpu.SemaphoreType.DMA(dims)


def slot_spec(slot):
    return pl.BlockSpec((SIDE, 1, TILE, FEAT), lambda step: (0, slot, 0, 0))


def call(kernel, name, outs, specs, operands, scratch, microseconds):
    return pl.pallas_call(
        kernel,
        grid=(1,),
        out_shape=outs,
        in_specs=specs,
        out_specs=tuple(VMEM for _ in outs) if isinstance(outs, tuple) else VMEM,
        scratch_shapes=scratch,
        compiler_params=PARAMS,
        cost_estimate=cost(microseconds),
        name=name,
    )(*operands)


def plane_copies(tiles, buffer, sems, z, offsets):
    copies = []
    for k, offset in enumerate(offsets):
        pair = []
        for yl in range(YLO):
            copy = pltpu.make_async_copy(
                tiles.at[yl, wrapped(z + offset)], buffer.at[k, yl], sems.at[k, yl]
            )
            copy.start()
            pair.append(copy)
        copies.append(pair)
    return copies


def far_forward_kernel(offsets, z_ref, src, weight, tiles, feats, out, buffer, sems):
    z = z_ref[0]
    copies = plane_copies(tiles, buffer, sems, z, offsets)
    for k, offset in enumerate(offsets):
        plane = wrapped(z + offset)
        for yl in range(YLO):
            copies[k][yl].wait()
            for x in range(NX):
                s = (yl * NZ + plane) * NX + x
                scale = weight[s].astype(F32) * 0.125
                product = dot(buffer[k, yl, x], feats[src[s]]) * scale
                out[yl * NX + x, k] = product.astype(BF16)


def far_forward(offsets, z, src, weight, tiles, feats):
    n = len(offsets)
    return call(
        functools.partial(far_forward_kernel, offsets),
        "far_forward",
        shape((SIDE, n, TILE, FEAT)),
        [SMEM, SMEM, SMEM, ANY, VMEM],
        (z, src, weight, tiles, feats),
        [pltpu.VMEM((n, YLO, NX, TILE, TILE), BF16), sems(n, YLO)],
        1 + n,
    )


def entry(table, z, plane, side):
    return table[plane, (side // NX * NZ + z) * NX + side % NX]


def add_arrived(acc, arrived, table, z, plane):
    for side in range(SIDE):
        j = entry(table, z, plane, side)
        acc[j] = acc[j] + arrived[side, 0].astype(F32)


def first_sum_kernel(z_ref, table, arrived, up, down, acc):
    z = z_ref[0]
    acc[...] = jnp.zeros(BLOCK_SET, F32)
    add_arrived(acc, arrived, table, z, wrapped(z + NZ // 2))
    up[...] = acc[: BLOCKS // 2].astype(BF16)
    down[...] = acc[BLOCKS // 2 :].astype(BF16)


def first_sum(slot, z, table, arrived):
    half = shape((BLOCKS // 2, TILE, FEAT))
    return call(
        first_sum_kernel,
        "first_sum",
        (half, half),
        [SMEM, SMEM, slot_spec(slot)],
        (z, table, arrived),
        [pltpu.VMEM(BLOCK_SET, F32)],
        2,
    )


def ring_sum_kernel(distance, z_ref, table, side_up, side_down, below, above, up, down, acc):
    z = z_ref[0]
    for sign, arrived, incoming, out in (
        (1, side_up, below, up),
        (-1, side_down, above, down),
    ):
        if incoming.shape[0] == BLOCKS:
            acc[...] = incoming[...].astype(F32)
        else:
            here = 0 if sign > 0 else BLOCKS // 2
            other = BLOCKS // 2 - here
            acc[here : here + BLOCKS // 2] = incoming[...].astype(F32)
            acc[other : other + BLOCKS // 2] = jnp.zeros((BLOCKS // 2, TILE, FEAT), F32)
        add_arrived(acc, arrived, table, z, wrapped(z + sign * distance))
        out[...] = acc[...].astype(BF16)


def ring_sum(distance, slots, z, table, arrived, below, above):
    return call(
        functools.partial(ring_sum_kernel, distance),
        "ring_sum",
        (shape(BLOCK_SET), shape(BLOCK_SET)),
        [SMEM, SMEM, slot_spec(slots[0]), slot_spec(slots[1]), VMEM, VMEM],
        (z, table, arrived, arrived, below, above),
        [pltpu.VMEM(BLOCK_SET, F32)],
        3,
    )


def group_copies(tiles, buffer, sems, rep_ids):
    copies = []
    for k, rep_id in enumerate(rep_ids):
        row = []
        for i in range(BLOCKS):
            copy = pltpu.make_async_copy(tiles.at[rep_id, i], buffer.at[k, i], sems.at[k, i])
            copy.start()
            row.append(copy)
        copies.append(row)
    return copies


def group_forward_kernel(n, reps, src, weight, tiles, *rest):
    feats, out, buffer, sems = rest[:n], rest[n], rest[n + 1], rest[n + 2]
    slots = buffer.shape[2]
    rep_ids = [reps[k] for k in range(n)]
    copies = group_copies(tiles, buffer, sems, rep_ids)
    for k in range(n):
        for i in range(BLOCKS):
            copies[k][i].wait()
            total = None
            for p in range(slots):
                index = (rep_ids[k] * BLOCKS + i) * slots + p
                scale = weight[index].astype(F32) * 0.125
                term = dot(buffer[k, i, p], feats[k][src[index]]) * scale
                total = term if total is None else total + term
            out[i] = total if k == 0 else out[i] + total


def group_forward(reps, src, weight, tiles, feats):
    n = len(feats)
    slots = tiles.shape[2]
    return call(
        functools.partial(group_forward_kernel, n),
        "group_forward",
        shape(BLOCK_SET, F32),
        [SMEM, SMEM, SMEM, ANY] + [VMEM] * n,
        (reps, src, weight, tiles, *feats),
        [pltpu.VMEM((n, BLOCKS, slots, TILE, TILE), BF16), sems(n, BLOCKS)],
        4 * n,
    )


def middle_kernel(
    z_ref, table, arrived, below, above, group_a, group_b, weight, cotangent,
    output, grad_agg, grad_weight, acc,
):
    z = z_ref[0]
    acc[...] = (
        group_a[...] + group_b[...] + below[...].astype(F32) + above[...].astype(F32)
    )
    add_arrived(acc, arrived, table, z, z)
    w = weight[...]
    step = 2
    total = None
    for i in range(0, BLOCKS, step):
        rows = pl.ds(i * TILE, step * TILE)
        agg = acc[i : i + step].reshape(step * TILE, FEAT).astype(BF16)
        pre = dot(agg, w)
        sig = 1.0 / (1.0 + jnp.exp(-pre))
        output[rows] = (pre * sig).astype(BF16)
        slope = sig * (1.0 + pre * (1.0 - sig))
        grad_pre = (cotangent[rows].astype(F32) * slope).astype(BF16)
        back = lax.dot_general(grad_pre, w, (((1,), (1,)), ((), ())), preferred_element_type=F32)
        grad_agg[i : i + step] = back.astype(BF16).reshape(step, TILE, FEAT)
        part = dot_t(agg, grad_pre)
        total = part if total is None else total + part
    high = total.astype(BF16)
    low = (total - high.astype(F32)).astype(BF16)
    grad_weight[:, :SLICE] = high.reshape(SIDE, SLICE, FEAT)
    grad_weight[:, SLICE:] = low.reshape(SIDE, SLICE, FEAT)


def middle(slot, z, table, arrived, below, above, group_a, group_b, weight, cotangent):
    return call(
        middle_kernel,
        "middle",
        (shape((BLOCKS * TILE, FEAT)), shape(BLOCK_SET), shape((SIDE, 2 * SLICE, FEAT))),
        [SMEM, SMEM, slot_spec(slot)] + [VMEM] * 6,
        (z, table, arrived, below, above, group_a, group_b, weight, cotangent),
        [pltpu.VMEM(BLOCK_SET, F32)],
        4,
    )


def select_kernel(offsets, halves, extra, z_ref, table, *rest):
    n = len(offsets)
    sources, out = rest[: n + halves], rest[-1]
    z = z_ref[0]
    half = BLOCKS // 2
    for k, offset in enumerate(offsets):
        plane = wrapped(z + offset)
        rows = pl.ds(k * TILE, TILE)
        for dest in range(SIDE):
            j = entry(table, z, plane, dest)
            if halves and k == n - 1:
                first = sources[k][jnp.minimum(j, half - 1)]
                second = sources[k + 1][jnp.maximum(j - half, 0)]
                out[dest, rows] = jnp.where(j < half, first, second)
            else:
                out[dest, rows] = sources[k][j]
    if extra:
        slices = rest[n + halves]
        for dest in range(SIDE):
            out[dest, n * TILE :] = slices[dest % extra]


def select(offsets, halves, z, table, sources, slices):
    n = len(offsets)
    extra = 0 if slices is None else slices.shape[0]
    operands = (z, table, *sources, *([slices] if extra else []))
    return call(
        functools.partial(select_kernel, offsets, halves, extra),
        "select",
        shape((SIDE, n * TILE + (2 * SLICE if extra else 0), FEAT)),
        [SMEM, SMEM] + [VMEM] * (len(operands) - 2),
        operands,
        [],
        2,
    )


def group_backward_kernel(n, has_start, reps, src, weight, tiles, grads, *rest):
    start = rest[0] if has_start else None
    out, buffer, sems, acc = rest[has_start:]
    slots = buffer.shape[2]
    rep_ids = [reps[k] for k in range(n)]
    copies = group_copies(tiles, buffer, sems, rep_ids)
    for k in range(n):
        if has_start:
            acc[...] = start[0].astype(F32)
        else:
            acc[...] = jnp.zeros(BLOCK_SET, F32)
        for i in range(BLOCKS):
            copies[k][i].wait()
            grad = grads[i]
            for p in range(slots):
                index = (rep_ids[k] * BLOCKS + i) * slots + p
                j = src[index]
                scale = weight[index].astype(F32) * 0.125
                acc[j] = acc[j] + dot_t(buffer[k, i, p], grad) * scale
        out[k] = acc[...].astype(out.dtype)


def group_backward(reps, n, dtype, src, weight, tiles, grads, start, slot):
    has_start = start is not None
    slots = tiles.shape[2]
    begin = pl.BlockSpec((1,) + BLOCK_SET, lambda step: (slot, 0, 0, 0))
    return call(
        functools.partial(group_backward_kernel, n, has_start),
        "group_backward",
        shape((n,) + BLOCK_SET, dtype),
        [SMEM, SMEM, SMEM, ANY, VMEM] + [begin] * has_start,
        (reps, src, weight, tiles, grads, *([start] if has_start else [])),
        [
            pltpu.VMEM((n, BLOCKS, slots, TILE, TILE), BF16),
            sems(n, BLOCKS),
            pltpu.VMEM(BLOCK_SET, F32),
        ],
        5 * n,
    )


def far_backward_kernel(offsets, extra, z_ref, src, weight, tiles, returned, start, *rest):
    more = rest[0] if extra else None
    out, buffer, sems, acc = rest[extra:]
    z = z_ref[0]
    copies = plane_copies(tiles, buffer, sems, z, offsets)
    acc[...] = start[...]
    if extra:
        acc[...] = acc[...] + more[...].astype(F32)
    for k, offset in enumerate(offsets):
        plane = wrapped(z + offset)
        for yl in range(YLO):
            copies[k][yl].wait()
            for x in range(NX):
                s = (yl * NZ + plane) * NX + x
                j = src[s]
                scale = weight[s].astype(F32) * 0.125
                grad = returned[yl * NX + x, pl.ds(k * TILE, TILE)]
                acc[j] = acc[j] + dot_t(buffer[k, yl, x], grad) * scale
    out[...] = acc[...].astype(out.dtype)


def far_backward(offsets, dtype, z, src, weight, tiles, returned, start, more):
    n = len(offsets)
    extra = more is not None
    return call(
        functools.partial(far_backward_kernel, offsets, extra),
        "far_backward",
        shape(BLOCK_SET, dtype),
        [SMEM, SMEM, SMEM, ANY, VMEM, VMEM] + [VMEM] * extra,
        (z, src, weight, tiles, returned, start, *([more] if extra else [])),
        [
            pltpu.VMEM((n, YLO, NX, TILE, TILE), BF16),
            sems(n, YLO),
            pltpu.VMEM(BLOCK_SET, F32),
        ],
        2 * n,
    )


def shift(value, axis, steps):
    count = lax.axis_size(axis)
    return lax.ppermute(value, axis, [(i, (i + steps) % count) for i in range(count)])


def meet(value, distance):
    return lax.ppermute(value, "z", [(i, i ^ distance) for i in range(NZ)])


def exchange(value, axis):
    return lax.all_to_all(value, axis, split_axis=0, concat_axis=0, tiled=True)


def after(value, *others):
    return lax.optimization_barrier((value, *others))[0]


SIDE_AXES = ("ylo", "x")


def per_device(
    features, weight, cotangent, group_tiles, group_src, group_wt,
    remote_tiles, remote_src, remote_wt, incoming_dst,
):
    z = lax.axis_index("z").astype(jnp.int32).reshape(1)
    yhi = lax.axis_index("yhi").astype(jnp.int32)
    core = lax.axis_index("core").astype(jnp.int32)

    def rep_of(other_yhi, other_core):
        return (yhi ^ other_yhi) * 2 + (core ^ other_core)

    feats = features.reshape(BLOCK_SET)
    tiles = group_tiles[0]
    src, wt = group_src.reshape(-1), group_wt.reshape(-1)
    far_tiles = remote_tiles.reshape(YLO, NZ, NX, TILE, TILE)
    far_src, far_wt = remote_src[0], remote_wt[0]
    table = exchange(jnp.tile(incoming_dst, (NZ, 1)), "z")

    def partials(offsets):
        return far_forward(offsets, z, far_src, far_wt, far_tiles, feats)

    def group_pair(other_yhi, own_core, other_core):
        reps = jnp.stack([rep_of(other_yhi, 0), rep_of(other_yhi, 1)])
        return group_forward(reps, src, wt, tiles, [own_core, other_core])

    sent_a = partials((4, 3, -3))
    got_a = exchange(after(sent_a, table), SIDE_AXES)
    feats_yhi = shift(feats, "yhi", 1)
    feats_core = shift(feats, "core", 1)
    sent_b = partials((2, -2))
    sent_c = partials((1, -1, 0))
    group_a = group_pair(0, feats, feats_core)
    feats_both = shift(feats_yhi, "core", 1)

    got_a = after(got_a, sent_b, sent_c, group_a)
    got_b = exchange(after(sent_b, got_a), SIDE_AXES)
    up, down = first_sum(0, z, table, got_a)
    below, above = shift(up, "z", 1), shift(down, "z", -1)
    up, down = ring_sum(3, (1, 2), z, table, got_a, below, above)
    below, above = shift(up, "z", 1), shift(down, "z", -1)
    got_c = exchange(after(sent_c, got_b), SIDE_AXES)
    group_b = group_pair(1, feats_yhi, feats_both)
    below, above = after((below, above), group_b)
    up, down = ring_sum(2, (0, 1), z, table, got_b, below, above)
    below, above = shift(up, "z", 1), shift(down, "z", -1)
    up, down = ring_sum(1, (0, 1), z, table, got_c, below, above)
    below, above = shift(up, "z", 1), shift(down, "z", -1)

    output, grads, grad_slices = middle(
        2, z, table, got_c, below, above, group_a, group_b, weight, cotangent
    )

    def group_term(reps, n, dtype, start, slot):
        return group_backward(reps, n, dtype, src, wt, tiles, grads, start, slot)

    def fold(offsets, dtype, returned, start, more):
        return far_backward(offsets, dtype, z, far_src, far_wt, far_tiles, returned, start, more)

    half = BLOCKS // 2
    below1, above1 = shift(grads, "z", 1), shift(grads, "z", -1)
    back_a = exchange(select((0,), False, z, table, [grads], grad_slices), SIDE_AXES)
    to_core = group_term(jnp.stack([rep_of(0, 1), rep_of(1, 1)]), 2, BF16, None, 0)

    below2, above2 = shift(below1, "z", 1), shift(above1, "z", -1)
    below1, above1 = after((below1, above1), to_core)
    chosen = select((-1, 1), False, z, table, [below1, above1], None)
    back_b = exchange(after(chosen, back_a), SIDE_AXES)
    from_core = shift(to_core, "core", 1)

    pairs = back_a[:, TILE:].astype(F32)
    part = jnp.sum(pairs[:, :SLICE] + pairs[:, SLICE:], axis=0)

    below3, above3 = shift(below2, "z", 1), shift(above2, "z", -1)
    to_yhi = group_term(rep_of(1, 0).reshape(1), 1, BF16, from_core, 1)
    from_yhi = shift(to_yhi[0], "yhi", 1)
    part = part + after(shift(part, "core", 1), to_yhi)
    below2, above2 = after((below2, above2), to_yhi)
    chosen = select((-2, 2), False, z, table, [below2, above2], None)
    back_c = exchange(after(chosen, back_b), SIDE_AXES)
    part = part + after(shift(part, "yhi", 1), chosen)

    below4, above4 = shift(below3[:half], "z", 1), shift(above3[half:], "z", -1)
    own = group_term(rep_of(0, 0).reshape(1), 1, F32, from_core, 0)[0]
    part = part + after(meet(part, 4), own)
    total = fold((0,), F32, back_a, own, from_yhi)
    part = part + after(meet(part, 1), total)
    below3, above3 = after((below3, above3), total)
    part = part + meet(part, 2)
    high = lax.reduce_precision(part, 8, 7)
    summed = jnp.concatenate([high, part - high], axis=0).astype(BF16)[None]
    chosen = select((-3, 3, 4), True, z, table, [below3, above3, below4, above4], summed)
    back_d = exchange(after(chosen, back_c), SIDE_AXES)
    total = fold((-1, 1), F32, back_b, total, None)
    total = fold((-2, 2), F32, back_c, total, None)
    back_d = after(back_d, total)
    grad_feat = fold((-3, 3, 4), BF16, back_d, total, None)
    pairs = back_d[:, 3 * TILE :].astype(F32)
    grad_weight = (pairs[:, :SLICE] + pairs[:, SLICE:]).reshape(FEAT, FEAT)
    grad_weight = grad_weight / math.sqrt(BLOCKS * TILE * math.prod(SIZES))
    return (output, grad_weight, grad_feat.reshape(BLOCKS * TILE, FEAT))


def solution(mesh):
    parts = Mesh(mesh.devices.reshape(SIZES), AXES)
    split = P(AXES)
    return jax.shard_map(
        per_device,
        mesh=parts,
        in_specs=(split, P(), split, split, split, split, split, split, split, split),
        out_specs=(split, P(), split),
        check_vma=False,
    )
```

```python
import functools
import math

import jax
import jax.numpy as jnp
from jax import lax
from jax.experimental import pallas as pl
from jax.experimental.pallas import tpu as pltpu
from jax.sharding import Mesh, PartitionSpec as P

AXES = ("ylo", "z", "x", "yhi", "core")
SIZES = (2, 8, 4, 2, 2)
YLO, NZ, NX = 2, 8, 4
SIDE = YLO * NX
BLOCKS, TILE, FEAT = 8, 128, 256
BF16, F32 = jnp.bfloat16, jnp.float32
VMEM = pl.BlockSpec(memory_space=pltpu.VMEM)
SMEM = pl.BlockSpec(memory_space=pltpu.SMEM)
ANY = pl.BlockSpec(memory_space=pl.ANY)
BLOCK_SET = (BLOCKS, TILE, FEAT)
SLICE = FEAT // SIDE
PARAMS = pltpu.CompilerParams(vmem_limit_bytes=56 * 1024 * 1024)


def dot(left, right):
    return jnp.dot(left, right, preferred_element_type=F32)


def dot_t(left, right):
    return lax.dot_general(left, right, (((0,), (0,)), ((), ())), preferred_element_type=F32)


def cost(microseconds):
    return pl.CostEstimate(
        flops=int(microseconds * 1e9), bytes_accessed=1024, transcendentals=0
    )


def wrapped(value):
    return lax.rem(value + NZ, NZ)


def shape(dims, dtype=BF16):
    return jax.ShapeDtypeStruct(dims, dtype)


def sems(*dims):
    return pltpu.SemaphoreType.DMA(dims)


def slot_spec(slot):
    return pl.BlockSpec((SIDE, 1, TILE, FEAT), lambda step: (0, slot, 0, 0))


def call(kernel, name, outs, specs, operands, scratch, microseconds):
    return pl.pallas_call(
        kernel,
        grid=(1,),
        out_shape=outs,
        in_specs=specs,
        out_specs=tuple(VMEM for _ in outs) if isinstance(outs, tuple) else VMEM,
        scratch_shapes=scratch,
        compiler_params=PARAMS,
        cost_estimate=cost(microseconds),
        name=name,
    )(*operands)


def plane_copies(tiles, buffer, sems, z, offsets):
    copies = []
    for k, offset in enumerate(offsets):
        pair = []
        for yl in range(YLO):
            copy = pltpu.make_async_copy(
                tiles.at[yl, wrapped(z + offset)], buffer.at[k, yl], sems.at[k, yl]
            )
            copy.start()
            pair.append(copy)
        copies.append(pair)
    return copies


def far_forward_kernel(offsets, z_ref, src, weight, tiles, feats, out, buffer, sems):
    z = z_ref[0]
    copies = plane_copies(tiles, buffer, sems, z, offsets)
    for k, offset in enumerate(offsets):
        plane = wrapped(z + offset)
        for yl in range(YLO):
            copies[k][yl].wait()
            for x in range(NX):
                s = (yl * NZ + plane) * NX + x
                scale = weight[s].astype(F32) * 0.125
                product = dot(buffer[k, yl, x], feats[src[s]]) * scale
                out[yl * NX + x, k] = product.astype(BF16)


def far_forward(offsets, z, src, weight, tiles, feats):
    n = len(offsets)
    return call(
        functools.partial(far_forward_kernel, offsets),
        "far_forward",
        shape((SIDE, n, TILE, FEAT)),
        [SMEM, SMEM, SMEM, ANY, VMEM],
        (z, src, weight, tiles, feats),
        [pltpu.VMEM((n, YLO, NX, TILE, TILE), BF16), sems(n, YLO)],
        1 + n,
    )


def entry(table, z, plane, side):
    return table[lax.bitwise_xor(plane, z), (side // NX * NZ + z) * NX + side % NX]


def add_arrived(acc, arrived, table, z, plane):
    for side in range(SIDE):
        j = entry(table, z, plane, side)
        acc[j] = acc[j] + arrived[side, 0].astype(F32)


def first_sum_kernel(z_ref, table, arrived, up, down, acc):
    z = z_ref[0]
    acc[...] = jnp.zeros(BLOCK_SET, F32)
    add_arrived(acc, arrived, table, z, wrapped(z + NZ // 2))
    up[...] = acc[: BLOCKS // 2].astype(BF16)
    down[...] = acc[BLOCKS // 2 :].astype(BF16)


def first_sum(slot, z, table, arrived):
    half = shape((BLOCKS // 2, TILE, FEAT))
    return call(
        first_sum_kernel,
        "first_sum",
        (half, half),
        [SMEM, SMEM, slot_spec(slot)],
        (z, table, arrived),
        [pltpu.VMEM(BLOCK_SET, F32)],
        2,
    )


def ring_sum_kernel(distance, z_ref, table, side_up, side_down, below, above, up, down, acc):
    z = z_ref[0]
    for sign, arrived, incoming, out in (
        (1, side_up, below, up),
        (-1, side_down, above, down),
    ):
        if incoming.shape[0] == BLOCKS:
            acc[...] = incoming[...].astype(F32)
        else:
            here = 0 if sign > 0 else BLOCKS // 2
            other = BLOCKS // 2 - here
            acc[here : here + BLOCKS // 2] = incoming[...].astype(F32)
            acc[other : other + BLOCKS // 2] = jnp.zeros((BLOCKS // 2, TILE, FEAT), F32)
        add_arrived(acc, arrived, table, z, wrapped(z + sign * distance))
        out[...] = acc[...].astype(BF16)


def ring_sum(distance, slots, z, table, arrived, below, above):
    return call(
        functools.partial(ring_sum_kernel, distance),
        "ring_sum",
        (shape(BLOCK_SET), shape(BLOCK_SET)),
        [SMEM, SMEM, slot_spec(slots[0]), slot_spec(slots[1]), VMEM, VMEM],
        (z, table, arrived, arrived, below, above),
        [pltpu.VMEM(BLOCK_SET, F32)],
        3,
    )


def group_copies(tiles, buffer, sems, rep_ids):
    copies = []
    for k, rep_id in enumerate(rep_ids):
        row = []
        for i in range(BLOCKS):
            copy = pltpu.make_async_copy(tiles.at[rep_id, i], buffer.at[k, i], sems.at[k, i])
            copy.start()
            row.append(copy)
        copies.append(row)
    return copies


def group_forward_kernel(n, reps, src, weight, tiles, *rest):
    feats, out, buffer, sems = rest[:n], rest[n], rest[n + 1], rest[n + 2]
    slots = buffer.shape[2]
    rep_ids = [reps[k] for k in range(n)]
    copies = group_copies(tiles, buffer, sems, rep_ids)
    for k in range(n):
        for i in range(BLOCKS):
            copies[k][i].wait()
            total = None
            for p in range(slots):
                index = (rep_ids[k] * BLOCKS + i) * slots + p
                scale = weight[index].astype(F32) * 0.125
                term = dot(buffer[k, i, p], feats[k][src[index]]) * scale
                total = term if total is None else total + term
            out[i] = total if k == 0 else out[i] + total


def group_forward(reps, src, weight, tiles, feats):
    n = len(feats)
    slots = tiles.shape[2]
    return call(
        functools.partial(group_forward_kernel, n),
        "group_forward",
        shape(BLOCK_SET, F32),
        [SMEM, SMEM, SMEM, ANY] + [VMEM] * n,
        (reps, src, weight, tiles, *feats),
        [pltpu.VMEM((n, BLOCKS, slots, TILE, TILE), BF16), sems(n, BLOCKS)],
        4 * n,
    )


def middle_kernel(
    z_ref, table, arrived, below, above, group_a, group_b, weight, cotangent,
    output, grad_agg, grad_weight, acc,
):
    z = z_ref[0]
    acc[...] = (
        group_a[...] + group_b[...] + below[...].astype(F32) + above[...].astype(F32)
    )
    add_arrived(acc, arrived, table, z, z)
    w = weight[...]
    step = 2
    total = None
    for i in range(0, BLOCKS, step):
        rows = pl.ds(i * TILE, step * TILE)
        agg = acc[i : i + step].reshape(step * TILE, FEAT).astype(BF16)
        pre = dot(agg, w)
        sig = 1.0 / (1.0 + jnp.exp(-pre))
        output[rows] = (pre * sig).astype(BF16)
        slope = sig * (1.0 + pre * (1.0 - sig))
        grad_pre = (cotangent[rows].astype(F32) * slope).astype(BF16)
        back = lax.dot_general(grad_pre, w, (((1,), (1,)), ((), ())), preferred_element_type=F32)
        grad_agg[i : i + step] = back.astype(BF16).reshape(step, TILE, FEAT)
        part = dot_t(agg, grad_pre)
        total = part if total is None else total + part
    high = total.astype(BF16)
    low = (total - high.astype(F32)).astype(BF16)
    grad_weight[:, :SLICE] = high.reshape(SIDE, SLICE, FEAT)
    grad_weight[:, SLICE:] = low.reshape(SIDE, SLICE, FEAT)


def middle(slot, z, table, arrived, below, above, group_a, group_b, weight, cotangent):
    return call(
        middle_kernel,
        "middle",
        (shape((BLOCKS * TILE, FEAT)), shape(BLOCK_SET), shape((SIDE, 2 * SLICE, FEAT))),
        [SMEM, SMEM, slot_spec(slot)] + [VMEM] * 6,
        (z, table, arrived, below, above, group_a, group_b, weight, cotangent),
        [pltpu.VMEM(BLOCK_SET, F32)],
        4,
    )


def select_kernel(offsets, halves, extra, z_ref, table, *rest):
    n = len(offsets)
    sources, out = rest[: n + halves], rest[-1]
    z = z_ref[0]
    half = BLOCKS // 2
    for k, offset in enumerate(offsets):
        plane = wrapped(z + offset)
        rows = pl.ds(k * TILE, TILE)
        for dest in range(SIDE):
            j = entry(table, z, plane, dest)
            if halves and k == n - 1:
                first = sources[k][jnp.minimum(j, half - 1)]
                second = sources[k + 1][jnp.maximum(j - half, 0)]
                out[dest, rows] = jnp.where(j < half, first, second)
            else:
                out[dest, rows] = sources[k][j]
    if extra:
        slices = rest[n + halves]
        for dest in range(SIDE):
            out[dest, n * TILE :] = slices[dest % extra]


def select(offsets, halves, z, table, sources, slices):
    n = len(offsets)
    extra = 0 if slices is None else slices.shape[0]
    operands = (z, table, *sources, *([slices] if extra else []))
    return call(
        functools.partial(select_kernel, offsets, halves, extra),
        "select",
        shape((SIDE, n * TILE + (2 * SLICE if extra else 0), FEAT)),
        [SMEM, SMEM] + [VMEM] * (len(operands) - 2),
        operands,
        [],
        2,
    )


def group_backward_kernel(n, has_start, reps, src, weight, tiles, grads, *rest):
    start = rest[0] if has_start else None
    out, buffer, sems, acc = rest[has_start:]
    slots = buffer.shape[2]
    rep_ids = [reps[k] for k in range(n)]
    copies = group_copies(tiles, buffer, sems, rep_ids)
    for k in range(n):
        if has_start:
            acc[...] = start[0].astype(F32)
        else:
            acc[...] = jnp.zeros(BLOCK_SET, F32)
        for i in range(BLOCKS):
            copies[k][i].wait()
            grad = grads[i]
            for p in range(slots):
                index = (rep_ids[k] * BLOCKS + i) * slots + p
                j = src[index]
                scale = weight[index].astype(F32) * 0.125
                acc[j] = acc[j] + dot_t(buffer[k, i, p], grad) * scale
        out[k] = acc[...].astype(out.dtype)


def group_backward(reps, n, dtype, src, weight, tiles, grads, start, slot):
    has_start = start is not None
    slots = tiles.shape[2]
    begin = pl.BlockSpec((1,) + BLOCK_SET, lambda step: (slot, 0, 0, 0))
    return call(
        functools.partial(group_backward_kernel, n, has_start),
        "group_backward",
        shape((n,) + BLOCK_SET, dtype),
        [SMEM, SMEM, SMEM, ANY, VMEM] + [begin] * has_start,
        (reps, src, weight, tiles, grads, *([start] if has_start else [])),
        [
            pltpu.VMEM((n, BLOCKS, slots, TILE, TILE), BF16),
            sems(n, BLOCKS),
            pltpu.VMEM(BLOCK_SET, F32),
        ],
        5 * n,
    )


def far_backward_kernel(groups, extra, z_ref, src, weight, tiles, start, *rest):
    returned = rest[: len(groups)]
    more = rest[len(groups)] if extra else None
    out, buffer, sems, acc = rest[len(groups) + extra :]
    z = z_ref[0]
    places = [(source, k) for source, group in zip(returned, groups) for k in range(len(group))]
    offsets = [offset for group in groups for offset in group]
    copies = plane_copies(tiles, buffer, sems, z, offsets)
    acc[...] = start[...]
    if extra:
        acc[...] = acc[...] + more[...].astype(F32)
    for at, (offset, (source, k)) in enumerate(zip(offsets, places)):
        plane = wrapped(z + offset)
        for yl in range(YLO):
            copies[at][yl].wait()
            for x in range(NX):
                s = (yl * NZ + plane) * NX + x
                j = src[s]
                scale = weight[s].astype(F32) * 0.125
                grad = source[yl * NX + x, pl.ds(k * TILE, TILE)]
                acc[j] = acc[j] + dot_t(buffer[at, yl, x], grad) * scale
    out[...] = acc[...].astype(out.dtype)


def far_backward(groups, dtype, z, src, weight, tiles, returned, start, more):
    n = sum(len(group) for group in groups)
    extra = more is not None
    return call(
        functools.partial(far_backward_kernel, groups, extra),
        "far_backward",
        shape(BLOCK_SET, dtype),
        [SMEM, SMEM, SMEM, ANY, VMEM] + [VMEM] * (len(groups) + extra),
        (z, src, weight, tiles, start, *returned, *([more] if extra else [])),
        [
            pltpu.VMEM((n, YLO, NX, TILE, TILE), BF16),
            sems(n, YLO),
            pltpu.VMEM(BLOCK_SET, F32),
        ],
        n,
    )


def shift(value, axis, steps):
    count = lax.axis_size(axis)
    return lax.ppermute(value, axis, [(i, (i + steps) % count) for i in range(count)])


def meet(value, distance):
    return lax.ppermute(value, "z", [(i, i ^ distance) for i in range(NZ)])


def exchange(value, axis):
    return lax.all_to_all(value, axis, split_axis=0, concat_axis=0, tiled=True)


def after(value, *others):
    return lax.optimization_barrier((value, *others))[0]


SIDE_AXES = ("ylo", "x")


def per_device(
    features, weight, cotangent, group_tiles, group_src, group_wt,
    remote_tiles, remote_src, remote_wt, incoming_dst,
):
    z = lax.axis_index("z").astype(jnp.int32).reshape(1)
    yhi = lax.axis_index("yhi").astype(jnp.int32)
    core = lax.axis_index("core").astype(jnp.int32)

    def rep_of(other_yhi, other_core):
        return (yhi ^ other_yhi) * 2 + (core ^ other_core)

    feats = features.reshape(BLOCK_SET)
    tiles = group_tiles[0]
    src, wt = group_src.reshape(-1), group_wt.reshape(-1)
    far_tiles = remote_tiles.reshape(YLO, NZ, NX, TILE, TILE)
    far_src, far_wt = remote_src[0], remote_wt[0]
    table = incoming_dst
    for bit in range(3):
        table = jnp.concatenate([table, meet(table, 1 << bit)], axis=0)

    def partials(offsets):
        return far_forward(offsets, z, far_src, far_wt, far_tiles, feats)

    def group_pair(other_yhi, own_core, other_core, earlier):
        reps = after(jnp.stack([rep_of(other_yhi, 0), rep_of(other_yhi, 1)]), earlier)
        return group_forward(reps, src, wt, tiles, [own_core, other_core])

    sent_a = partials((4, 3, -3))
    got_a = exchange(sent_a, SIDE_AXES)
    feats_yhi = shift(feats, "yhi", 1)
    feats_core = shift(feats, "core", 1)
    sent_b = partials((2, -2))
    sent_c = partials((1, -1, 0))

    got_a = after(got_a, sent_b, sent_c, table)
    got_b = exchange(after(sent_b, got_a), SIDE_AXES)
    up, down = first_sum(0, z, table, got_a)
    below, above = shift(up, "z", 1), shift(down, "z", -1)
    up, down = ring_sum(3, (1, 2), z, table, got_a, below, above)
    below, above = shift(up, "z", 1), shift(down, "z", -1)
    got_c = exchange(after(sent_c, got_b), SIDE_AXES)
    up, down = ring_sum(2, (0, 1), z, table, got_b, below, above)
    below, above = shift(up, "z", 1), shift(down, "z", -1)
    group_a = group_pair(0, feats, feats_core, up)
    below, above = after((below, above), group_a)
    up, down = ring_sum(1, (0, 1), z, table, got_c, below, above)
    below, above = shift(up, "z", 1), shift(down, "z", -1)
    feats_yhi = after(feats_yhi, up)
    feats_both = shift(feats_yhi, "core", 1)
    group_b = group_pair(1, feats_yhi, feats_both, up)

    output, grads, grad_slices = middle(
        2, z, table, got_c, below, above, group_a, group_b, weight, cotangent
    )

    def group_term(reps, n, dtype, start, slot):
        return group_backward(reps, n, dtype, src, wt, tiles, grads, start, slot)

    def fold(groups, dtype, returned, start, more):
        return far_backward(groups, dtype, z, far_src, far_wt, far_tiles, returned, start, more)

    half = BLOCKS // 2
    below1, above1 = shift(grads, "z", 1), shift(grads, "z", -1)
    chosen = select((0,), False, z, table, [grads], grad_slices)
    back_a = exchange(chosen, SIDE_AXES)
    reps = after(jnp.stack([rep_of(0, 1), rep_of(1, 1)]), below1, above1)
    to_core = group_term(reps, 2, BF16, None, 0)

    below2, above2 = shift(below1, "z", 1), shift(above1, "z", -1)
    chosen = select((-1, 1), False, z, table, [below1, above1], None)
    back_b = exchange(after(chosen, back_a), SIDE_AXES)
    from_core = shift(to_core, "core", 1)

    pairs = back_a[:, TILE:].astype(F32)
    part = jnp.sum(pairs[:, :SLICE] + pairs[:, SLICE:], axis=0)
    part = part + after(shift(part, "core", 1), to_core)

    below2, above2 = after((below2, above2), to_core)
    below3, above3 = shift(below2, "z", 1), shift(above2, "z", -1)
    to_yhi = group_term(after(rep_of(1, 0).reshape(1), part), 1, BF16, from_core, 1)
    from_yhi = shift(to_yhi[0], "yhi", 1)
    below2, above2 = after((below2, above2), to_yhi)
    chosen = select((-2, 2), False, z, table, [below2, above2], None)
    back_c = exchange(after(chosen, back_b), SIDE_AXES)

    below4, above4 = shift(below3[:half], "z", 1), shift(above3[half:], "z", -1)
    chosen = select((-3, 3, 4), True, z, table, [below3, above3, below4, above4], None)
    part = part + after(meet(part, 4), chosen)
    back_d = exchange(after(chosen, back_c), SIDE_AXES)
    reps = after(rep_of(0, 0).reshape(1), chosen, from_yhi)
    own = group_term(reps, 1, F32, from_core, 0)[0]
    part = part + after(meet(part, 1), own)
    total = fold(((0,), (-1, 1)), F32, [back_a, back_b], own, from_yhi)
    part = part + after(meet(part, 2), total)
    total = fold(((-2, 2),), F32, [back_c], total, None)
    part = part + after(shift(part, "yhi", 1), total)
    part = part / math.sqrt(BLOCKS * TILE * math.prod(SIZES))
    back_d = after(back_d, total, part)
    grad_weight = exchange(after(jnp.tile(part, (SIDE, 1)), back_d), SIDE_AXES)
    grad_feat = fold(((-3, 3, 4),), BF16, [back_d], total, None)
    return (output, grad_weight, grad_feat.reshape(BLOCKS * TILE, FEAT))


def solution(mesh):
    parts = Mesh(mesh.devices.reshape(SIZES), AXES)
    split = P(AXES)
    return jax.shard_map(
        per_device,
        mesh=parts,
        in_specs=(split, P(), split, split, split, split, split, split, split, split),
        out_specs=(split, P(), split),
        check_vma=False,
    )
```

```python
import functools
import math

import jax
import jax.numpy as jnp
from jax import lax
from jax.experimental import pallas as pl
from jax.experimental.pallas import tpu as pltpu
from jax.sharding import Mesh, PartitionSpec as P

AXES = ("ylo", "z", "x", "yhi", "core")
SIZES = (2, 8, 4, 2, 2)
YLO, NZ, NX = 2, 8, 4
SIDE = YLO * NX
BLOCKS, TILE, FEAT = 8, 128, 256
BF16, F32 = jnp.bfloat16, jnp.float32
VMEM = pl.BlockSpec(memory_space=pltpu.VMEM)
SMEM = pl.BlockSpec(memory_space=pltpu.SMEM)
ANY = pl.BlockSpec(memory_space=pl.ANY)
BLOCK_SET = (BLOCKS, TILE, FEAT)
SLICE = FEAT // SIDE
PARAMS = pltpu.CompilerParams(vmem_limit_bytes=56 * 1024 * 1024)


def dot(left, right):
    return jnp.dot(left, right, preferred_element_type=F32)


def dot_t(left, right):
    return lax.dot_general(left, right, (((0,), (0,)), ((), ())), preferred_element_type=F32)


def cost(microseconds):
    return pl.CostEstimate(
        flops=int(microseconds * 1e9), bytes_accessed=1024, transcendentals=0
    )


def wrapped(value):
    return lax.rem(value + NZ, NZ)


def shape(dims, dtype=BF16):
    return jax.ShapeDtypeStruct(dims, dtype)


def sems(*dims):
    return pltpu.SemaphoreType.DMA(dims)


def slot_spec(slot):
    return pl.BlockSpec((SIDE, 1, TILE, FEAT), lambda step: (0, slot, 0, 0))


def call(kernel, name, outs, specs, operands, scratch, microseconds):
    return pl.pallas_call(
        kernel,
        grid=(1,),
        out_shape=outs,
        in_specs=specs,
        out_specs=tuple(VMEM for _ in outs) if isinstance(outs, tuple) else VMEM,
        scratch_shapes=scratch,
        compiler_params=PARAMS,
        cost_estimate=cost(microseconds),
        name=name,
    )(*operands)


def plane_copies(tiles, buffer, sems, z, offsets):
    copies = []
    for k, offset in enumerate(offsets):
        pair = []
        for yl in range(YLO):
            copy = pltpu.make_async_copy(
                tiles.at[yl, wrapped(z + offset)], buffer.at[k, yl], sems.at[k, yl]
            )
            copy.start()
            pair.append(copy)
        copies.append(pair)
    return copies


def far_forward_kernel(offsets, z_ref, src, weight, tiles, feats, out, buffer, sems):
    z = z_ref[0]
    copies = plane_copies(tiles, buffer, sems, z, offsets)
    for k, offset in enumerate(offsets):
        plane = wrapped(z + offset)
        for yl in range(YLO):
            copies[k][yl].wait()
            for x in range(NX):
                s = (yl * NZ + plane) * NX + x
                scale = weight[s].astype(F32) * 0.125
                product = dot(buffer[k, yl, x], feats[src[s]]) * scale
                out[yl * NX + x, k] = product.astype(BF16)


def far_forward(offsets, z, src, weight, tiles, feats):
    n = len(offsets)
    return call(
        functools.partial(far_forward_kernel, offsets),
        "far_forward",
        shape((SIDE, n, TILE, FEAT)),
        [SMEM, SMEM, SMEM, ANY, VMEM],
        (z, src, weight, tiles, feats),
        [pltpu.VMEM((n, YLO, NX, TILE, TILE), BF16), sems(n, YLO)],
        1 + n,
    )


def entry(table, z, plane, side):
    return table[lax.bitwise_xor(plane, z), (side // NX * NZ + z) * NX + side % NX]


def add_arrived(acc, arrived, table, z, plane):
    for side in range(SIDE):
        j = entry(table, z, plane, side)
        acc[j] = acc[j] + arrived[side, 0].astype(F32)


def first_sum_kernel(z_ref, table, arrived, up, down, acc):
    z = z_ref[0]
    acc[...] = jnp.zeros(BLOCK_SET, F32)
    add_arrived(acc, arrived, table, z, wrapped(z + NZ // 2))
    up[...] = acc[: BLOCKS // 2].astype(BF16)
    down[...] = acc[BLOCKS // 2 :].astype(BF16)


def first_sum(slot, z, table, arrived):
    half = shape((BLOCKS // 2, TILE, FEAT))
    return call(
        first_sum_kernel,
        "first_sum",
        (half, half),
        [SMEM, SMEM, slot_spec(slot)],
        (z, table, arrived),
        [pltpu.VMEM(BLOCK_SET, F32)],
        2,
    )


def ring_sum_kernel(distance, z_ref, table, side_up, side_down, below, above, up, down, acc):
    z = z_ref[0]
    for sign, arrived, incoming, out in (
        (1, side_up, below, up),
        (-1, side_down, above, down),
    ):
        if incoming.shape[0] == BLOCKS:
            acc[...] = incoming[...].astype(F32)
        else:
            here = 0 if sign > 0 else BLOCKS // 2
            other = BLOCKS // 2 - here
            acc[here : here + BLOCKS // 2] = incoming[...].astype(F32)
            acc[other : other + BLOCKS // 2] = jnp.zeros((BLOCKS // 2, TILE, FEAT), F32)
        add_arrived(acc, arrived, table, z, wrapped(z + sign * distance))
        out[...] = acc[...].astype(BF16)


def ring_sum(distance, slots, z, table, arrived, below, above):
    return call(
        functools.partial(ring_sum_kernel, distance),
        "ring_sum",
        (shape(BLOCK_SET), shape(BLOCK_SET)),
        [SMEM, SMEM, slot_spec(slots[0]), slot_spec(slots[1]), VMEM, VMEM],
        (z, table, arrived, arrived, below, above),
        [pltpu.VMEM(BLOCK_SET, F32)],
        3,
    )


def group_copies(tiles, buffer, sems, rep_ids):
    copies = []
    for k, rep_id in enumerate(rep_ids):
        row = []
        for i in range(BLOCKS):
            copy = pltpu.make_async_copy(tiles.at[rep_id, i], buffer.at[k, i], sems.at[k, i])
            copy.start()
            row.append(copy)
        copies.append(row)
    return copies


def group_forward_kernel(n, reps, src, weight, tiles, *rest):
    feats, out, buffer, sems = rest[:n], rest[n], rest[n + 1], rest[n + 2]
    slots = buffer.shape[2]
    rep_ids = [reps[k] for k in range(n)]
    copies = group_copies(tiles, buffer, sems, rep_ids)
    for k in range(n):
        for i in range(BLOCKS):
            copies[k][i].wait()
            total = None
            for p in range(slots):
                index = (rep_ids[k] * BLOCKS + i) * slots + p
                scale = weight[index].astype(F32) * 0.125
                term = dot(buffer[k, i, p], feats[k][src[index]]) * scale
                total = term if total is None else total + term
            out[i] = total if k == 0 else out[i] + total


def group_forward(reps, src, weight, tiles, feats):
    n = len(feats)
    slots = tiles.shape[2]
    return call(
        functools.partial(group_forward_kernel, n),
        "group_forward",
        shape(BLOCK_SET, F32),
        [SMEM, SMEM, SMEM, ANY] + [VMEM] * n,
        (reps, src, weight, tiles, *feats),
        [pltpu.VMEM((n, BLOCKS, slots, TILE, TILE), BF16), sems(n, BLOCKS)],
        4 * n,
    )


def middle_kernel(
    z_ref, table, arrived, below, above, group_a, group_b, weight, cotangent,
    output, grad_agg, grad_weight, acc,
):
    z = z_ref[0]
    acc[...] = (
        group_a[...] + group_b[...] + below[...].astype(F32) + above[...].astype(F32)
    )
    add_arrived(acc, arrived, table, z, z)
    w = weight[...]
    step = 2
    total = None
    for i in range(0, BLOCKS, step):
        rows = pl.ds(i * TILE, step * TILE)
        agg = acc[i : i + step].reshape(step * TILE, FEAT).astype(BF16)
        pre = dot(agg, w)
        sig = 1.0 / (1.0 + jnp.exp(-pre))
        output[rows] = (pre * sig).astype(BF16)
        slope = sig * (1.0 + pre * (1.0 - sig))
        grad_pre = (cotangent[rows].astype(F32) * slope).astype(BF16)
        back = lax.dot_general(grad_pre, w, (((1,), (1,)), ((), ())), preferred_element_type=F32)
        grad_agg[i : i + step] = back.astype(BF16).reshape(step, TILE, FEAT)
        part = dot_t(agg, grad_pre)
        total = part if total is None else total + part
    high = total.astype(BF16)
    low = (total - high.astype(F32)).astype(BF16)
    grad_weight[:, :SLICE] = high.reshape(SIDE, SLICE, FEAT)
    grad_weight[:, SLICE:] = low.reshape(SIDE, SLICE, FEAT)


def middle(slot, z, table, arrived, below, above, group_a, group_b, weight, cotangent):
    return call(
        middle_kernel,
        "middle",
        (shape((BLOCKS * TILE, FEAT)), shape(BLOCK_SET), shape((SIDE, 2 * SLICE, FEAT))),
        [SMEM, SMEM, slot_spec(slot)] + [VMEM] * 6,
        (z, table, arrived, below, above, group_a, group_b, weight, cotangent),
        [pltpu.VMEM(BLOCK_SET, F32)],
        4,
    )


def select_kernel(offsets, halves, extra, z_ref, table, *rest):
    n = len(offsets)
    sources, out = rest[: n + halves], rest[-1]
    z = z_ref[0]
    half = BLOCKS // 2
    for k, offset in enumerate(offsets):
        plane = wrapped(z + offset)
        rows = pl.ds(k * TILE, TILE)
        for dest in range(SIDE):
            j = entry(table, z, plane, dest)
            if halves and k == n - 1:
                first = sources[k][jnp.minimum(j, half - 1)]
                second = sources[k + 1][jnp.maximum(j - half, 0)]
                out[dest, rows] = jnp.where(j < half, first, second)
            else:
                out[dest, rows] = sources[k][j]
    if extra:
        slices = rest[n + halves]
        for dest in range(SIDE):
            out[dest, n * TILE :] = slices[dest % extra]


def select(offsets, halves, z, table, sources, slices):
    n = len(offsets)
    extra = 0 if slices is None else slices.shape[0]
    operands = (z, table, *sources, *([slices] if extra else []))
    return call(
        functools.partial(select_kernel, offsets, halves, extra),
        "select",
        shape((SIDE, n * TILE + (2 * SLICE if extra else 0), FEAT)),
        [SMEM, SMEM] + [VMEM] * (len(operands) - 2),
        operands,
        [],
        2,
    )


def group_backward_kernel(n, has_start, reps, src, weight, tiles, grads, *rest):
    start = rest[0] if has_start else None
    out, buffer, sems, acc = rest[has_start:]
    slots = buffer.shape[2]
    rep_ids = [reps[k] for k in range(n)]
    copies = group_copies(tiles, buffer, sems, rep_ids)
    for k in range(n):
        if has_start:
            acc[...] = start[0].astype(F32)
        else:
            acc[...] = jnp.zeros(BLOCK_SET, F32)
        for i in range(BLOCKS):
            copies[k][i].wait()
            grad = grads[i]
            for p in range(slots):
                index = (rep_ids[k] * BLOCKS + i) * slots + p
                j = src[index]
                scale = weight[index].astype(F32) * 0.125
                acc[j] = acc[j] + dot_t(buffer[k, i, p], grad) * scale
        out[k] = acc[...].astype(out.dtype)


def group_backward(reps, n, dtype, src, weight, tiles, grads, start, slot):
    has_start = start is not None
    slots = tiles.shape[2]
    begin = pl.BlockSpec((1,) + BLOCK_SET, lambda step: (slot, 0, 0, 0))
    return call(
        functools.partial(group_backward_kernel, n, has_start),
        "group_backward",
        shape((n,) + BLOCK_SET, dtype),
        [SMEM, SMEM, SMEM, ANY, VMEM] + [begin] * has_start,
        (reps, src, weight, tiles, grads, *([start] if has_start else [])),
        [
            pltpu.VMEM((n, BLOCKS, slots, TILE, TILE), BF16),
            sems(n, BLOCKS),
            pltpu.VMEM(BLOCK_SET, F32),
        ],
        5 * n,
    )


def far_backward_kernel(groups, extra, first, z_ref, src, weight, tiles, start, *rest):
    returned = rest[: len(groups)]
    more = rest[len(groups)] if extra else None
    out, buffer, sems, acc = rest[len(groups) + extra :]
    z = z_ref[0]
    places = [(source, k) for source, group in zip(returned, groups) for k in range(len(group))]
    offsets = [offset for group in groups for offset in group]
    copies = plane_copies(tiles, buffer, sems, z, offsets)
    acc[...] = start[...]
    if extra:
        last = first + more.shape[0]
        acc[first:last] = acc[first:last] + more[...].astype(F32)
    for at, (offset, (source, k)) in enumerate(zip(offsets, places)):
        plane = wrapped(z + offset)
        for yl in range(YLO):
            copies[at][yl].wait()
            for x in range(NX):
                s = (yl * NZ + plane) * NX + x
                j = src[s]
                scale = weight[s].astype(F32) * 0.125
                grad = source[yl * NX + x, pl.ds(k * TILE, TILE)]
                acc[j] = acc[j] + dot_t(buffer[at, yl, x], grad) * scale
    out[...] = acc[...].astype(out.dtype)


def far_backward(groups, dtype, z, src, weight, tiles, returned, start, more, first):
    n = sum(len(group) for group in groups)
    extra = more is not None
    return call(
        functools.partial(far_backward_kernel, groups, extra, first),
        "far_backward",
        shape(BLOCK_SET, dtype),
        [SMEM, SMEM, SMEM, ANY, VMEM] + [VMEM] * (len(groups) + extra),
        (z, src, weight, tiles, start, *returned, *([more] if extra else [])),
        [
            pltpu.VMEM((n, YLO, NX, TILE, TILE), BF16),
            sems(n, YLO),
            pltpu.VMEM(BLOCK_SET, F32),
        ],
        n,
    )


def shift(value, axis, steps):
    count = lax.axis_size(axis)
    return lax.ppermute(value, axis, [(i, (i + steps) % count) for i in range(count)])


def meet(value, distance):
    return lax.ppermute(value, "z", [(i, i ^ distance) for i in range(NZ)])


def exchange(value, axis):
    return lax.all_to_all(value, axis, split_axis=0, concat_axis=0, tiled=True)


def after(value, *others):
    return lax.optimization_barrier((value, *others))[0]


SIDE_AXES = ("ylo", "x")


def per_device(
    features, weight, cotangent, group_tiles, group_src, group_wt,
    remote_tiles, remote_src, remote_wt, incoming_dst,
):
    z = lax.axis_index("z").astype(jnp.int32).reshape(1)
    yhi = lax.axis_index("yhi").astype(jnp.int32)
    core = lax.axis_index("core").astype(jnp.int32)

    def rep_of(other_yhi, other_core):
        return (yhi ^ other_yhi) * 2 + (core ^ other_core)

    feats = features.reshape(BLOCK_SET)
    tiles = group_tiles[0]
    src, wt = group_src.reshape(-1), group_wt.reshape(-1)
    far_tiles = remote_tiles.reshape(YLO, NZ, NX, TILE, TILE)
    far_src, far_wt = remote_src[0], remote_wt[0]
    table = incoming_dst
    for bit in range(3):
        table = jnp.concatenate([table, meet(table, 1 << bit)], axis=0)

    def partials(offsets):
        return far_forward(offsets, z, far_src, far_wt, far_tiles, feats)

    def group_pair(other_yhi, own_core, other_core, earlier):
        reps = after(jnp.stack([rep_of(other_yhi, 0), rep_of(other_yhi, 1)]), earlier)
        return group_forward(reps, src, wt, tiles, [own_core, other_core])

    sent_a = partials((4, 3, -3))
    got_a = exchange(sent_a, SIDE_AXES)
    feats_yhi = shift(feats, "yhi", 1)
    feats_core = shift(feats, "core", 1)
    sent_b = partials((2, -2))
    sent_c = partials((1, -1, 0))

    got_a = after(got_a, sent_b, sent_c, table)
    got_b = exchange(after(sent_b, got_a), SIDE_AXES)
    up, down = first_sum(0, z, table, got_a)
    below, above = shift(up, "z", 1), shift(down, "z", -1)
    up, down = ring_sum(3, (1, 2), z, table, got_a, below, above)
    below, above = shift(up, "z", 1), shift(down, "z", -1)
    got_c = exchange(after(sent_c, got_b), SIDE_AXES)
    up, down = ring_sum(2, (0, 1), z, table, got_b, below, above)
    below, above = shift(up, "z", 1), shift(down, "z", -1)
    group_a = group_pair(0, feats, feats_core, up)
    below, above = after((below, above), group_a)
    up, down = ring_sum(1, (0, 1), z, table, got_c, below, above)
    below, above = shift(up, "z", 1), shift(down, "z", -1)
    feats_yhi = after(feats_yhi, up)
    feats_both = shift(feats_yhi, "core", 1)
    group_b = group_pair(1, feats_yhi, feats_both, up)

    output, grads, grad_slices = middle(
        2, z, table, got_c, below, above, group_a, group_b, weight, cotangent
    )

    def group_term(reps, n, dtype, start, slot):
        return group_backward(reps, n, dtype, src, wt, tiles, grads, start, slot)

    def fold(groups, dtype, returned, start, more, first):
        return far_backward(
            groups, dtype, z, far_src, far_wt, far_tiles, returned, start, more, first
        )

    half = BLOCKS // 2
    below1, above1 = shift(grads, "z", 1), shift(grads, "z", -1)
    chosen = select((0,), False, z, table, [grads], grad_slices)
    back_a = exchange(chosen, SIDE_AXES)
    reps = after(jnp.stack([rep_of(0, 1), rep_of(1, 1)]), below1, above1)
    to_core = group_term(reps, 2, BF16, None, 0)

    below2, above2 = shift(below1, "z", 1), shift(above1, "z", -1)
    chosen = select((-1, 1), False, z, table, [below1, above1], None)
    back_b = exchange(after(chosen, back_a), SIDE_AXES)
    from_core = shift(to_core, "core", 1)

    pairs = back_a[:, TILE:].astype(F32)
    part = jnp.sum(pairs[:, :SLICE] + pairs[:, SLICE:], axis=0)
    part = part + after(shift(part, "core", 1), to_core)

    below2, above2 = after((below2, above2), to_core)
    below3, above3 = shift(below2, "z", 1), shift(above2, "z", -1)
    to_yhi = group_term(after(rep_of(1, 0).reshape(1), part), 1, BF16, from_core, 1)
    from_low, from_high = shift(to_yhi[0, :half], "yhi", 1), shift(to_yhi[0, half:], "yhi", 1)
    below2, above2 = after((below2, above2), to_yhi)
    chosen = select((-2, 2), False, z, table, [below2, above2], None)
    back_c = exchange(after(chosen, back_b), SIDE_AXES)

    below4, above4 = shift(below3[:half], "z", 1), shift(above3[half:], "z", -1)
    chosen = select((-3, 3, 4), True, z, table, [below3, above3, below4, above4], None)
    part = part + after(meet(part, 4), chosen)
    back_d = exchange(after(chosen, back_c), SIDE_AXES)
    reps = after(rep_of(0, 0).reshape(1), chosen, from_low)
    own = group_term(reps, 1, F32, from_core, 0)[0]
    part = part + after(meet(part, 1), own)
    total = fold(((0,), (-1, 1)), F32, [back_a, back_b], own, from_low, 0)
    part = part + after(meet(part, 2), total)
    total = fold(((-2, 2),), F32, [back_c], total, from_high, half)
    part = part + after(shift(part, "yhi", 1), total)
    part = part / math.sqrt(BLOCKS * TILE * math.prod(SIZES))
    back_d = after(back_d, total, part)
    grad_weight = exchange(after(jnp.tile(part, (SIDE, 1)), back_d), SIDE_AXES)
    grad_feat = fold(((-3, 3, 4),), BF16, [back_d], total, None, 0)
    return (output, grad_weight, grad_feat.reshape(BLOCKS * TILE, FEAT))


def solution(mesh):
    parts = Mesh(mesh.devices.reshape(SIZES), AXES)
    split = P(AXES)
    return jax.shard_map(
        per_device,
        mesh=parts,
        in_specs=(split, P(), split, split, split, split, split, split, split, split),
        out_specs=(split, P(), split),
        check_vma=False,
    )
```
